256 devices in a mesh: view: 64 (over z, x, core), seq: 4 (over y).
Axes of the slice: x: 4, y: 4, z: 8, core: 2. Of those that a mesh axis runs over, the one named last changes fastest.
Arguments:
- queries: bfloat16 [64, 768, 1024], P('view', 'seq'), may hold values from -6 to 6
- keys: bfloat16 [64, 768, 1024], P('view', 'seq'), may hold values from -6 to 6
- values: bfloat16 [64, 768, 1024], P('view', 'seq'), may hold values from -6 to 6
- out_grad: bfloat16 [64, 768, 1024], P('view', 'seq'), may hold values from -6 to 6
- nbr_views: int32 [64, 3], P('view'), may hold values from 0 to 63, as said below
- nbr_counts: int32 [64], P('view'), may hold values from 1 to 3, as said below
Outputs:
- attended: bfloat16 [64, 768, 1024], P('view', 'seq')
- grad_q: bfloat16 [64, 768, 1024], P('view', 'seq')
- grad_k: bfloat16 [64, 768, 1024], P('view', 'seq')
- grad_v: bfloat16 [64, 768, 1024], P('view', 'seq')
The draws below stay inside these ranges and needn't reach their ends.
Inputs may be any that keep to these rules, and one draw needn't show every extreme that they name: `nbr_views`: views v with equal v // 16 form a scene. The 3 entries of view v's list are distinct views of v's scene, other than v, at most 4 views away from v. Only the first nbr_counts[v] entries of view v's list are its neighbours.
All inputs are finite; a program needn't handle non-finite values.
Results may differ from the reference program's by a relative error of at most 0.034.
Values may be sent and summed in bfloat16 or wider, within the bound.
No kernel may reach another device: no remote copies, remote signals or barrier semaphores. Data moves between devices by JAX's collectives and lax.ppermute only.
A program may use at most 128 MiB of HBM per device.

```python
import jax
import jax.numpy as jnp
from jax import lax

HEADS = 16
HEAD_DIM = 64
HD = 1024
TOK_VIEW = 768
VIEWS = 64
SCENE = 16
RADIUS = 4
MAXNB = 3


def draw_queries(key, part):
    key = jax.random.fold_in(key, 3)
    rough = jnp.clip(jax.random.normal(key, (VIEWS, TOK_VIEW, HD), jnp.float32), -6.0, 6.0)
    return rough.astype(jnp.bfloat16)


def draw_keys(key, part):
    key = jax.random.fold_in(key, 5)
    rough = jnp.clip(jax.random.normal(key, (VIEWS, TOK_VIEW, HD), jnp.float32), -6.0, 6.0)
    return rough.astype(jnp.bfloat16)


def draw_nbr_views(key, part):
    key = jax.random.fold_in(key, 7)
    width = 2 * RADIUS
    steps_all = jnp.concatenate([jnp.arange(-RADIUS, 0, dtype=jnp.int32), jnp.arange(1, RADIUS + 1, dtype=jnp.int32)])
    own_views = jnp.arange(VIEWS, dtype=jnp.int32)
    position = own_views % SCENE
    landing = position[:, None] + steps_all[None, :]
    usable = (landing >= 0) & (landing < SCENE)
    random_rank = jax.random.randint(key, (VIEWS, width), 0, 1 << 20)
    ranking = random_rank * width + jnp.arange(width, dtype=jnp.int32)[None, :]
    ranking = jnp.where(usable, ranking, ranking + (1 << 28))
    forced = (position == SCENE - 2)[:, None] & (steps_all[None, :] == 1) | (position == 1)[:, None] & (steps_all[None, :] == -1)
    ranking = jnp.where(forced, -1, ranking)
    order = jnp.argsort(ranking, axis=1, stable=True)
    targets = own_views[:, None] + steps_all[None, :]
    return jnp.take_along_axis(targets, order[:, :MAXNB], axis=1).astype(jnp.int32)


def draw_nbr_counts(key, part):
    key = jax.random.fold_in(key, 11)
    first_key, second_key = jax.random.split(key)
    counts = jax.random.randint(first_key, (VIEWS,), 1, MAXNB + 1)
    chosen = jax.random.randint(second_key, (), 0, SCENE)
    position = jnp.arange(VIEWS, dtype=jnp.int32) % SCENE
    counts = jnp.where(position == chosen, MAXNB, counts)
    counts = jnp.where(position == (chosen + 1) % SCENE, 1, counts)
    return counts.astype(jnp.int32)


def level_of(key, shape, cuts, smallest, high):
    def one(axis_at, parts):
        draws = jax.random.uniform(jax.random.fold_in(jax.random.fold_in(key, 6), axis_at), (parts,), jnp.float32, smallest / len(cuts), high / len(cuts))
        return jnp.repeat(jnp.exp(draws), shape[axis_at] // parts).reshape((-1,) + (1,) * (len(shape) - axis_at - 1))

    loudness = one(*cuts[0])
    for cut in cuts[1:]:
        loudness = loudness * one(*cut)
    return loudness


def centred(rng, extent, spread, limit, pieces=(), kind=jnp.bfloat16):
    array = spread * jax.random.normal(rng, extent, jnp.float32)
    if pieces:
        array = array * level_of(rng, extent, pieces, -0.22, 0.18)
    return jnp.clip(array, -limit, limit).astype(kind)


def setup_inputs(seed: int = 0) -> dict:
    key_list = jax.random.split(jax.random.key(seed), 7)
    return {
        "queries": draw_queries(jax.random.fold_in(key_list[6], 71), 0),
        "keys": draw_keys(jax.random.fold_in(key_list[6], 71), 0),
        "values": centred(key_list[2], (VIEWS, TOK_VIEW, HD), 1.0, 6.0, ((0, 64), (1, 4))),
        "out_grad": centred(key_list[3], (VIEWS, TOK_VIEW, HD), 1.0, 6.0, ((0, 64), (1, 4))),
        "nbr_views": draw_nbr_views(jax.random.fold_in(key_list[6], 71), 0),
        "nbr_counts": draw_nbr_counts(jax.random.fold_in(key_list[6], 71), 0),
    }


def reference(queries, keys, values, out_grad, nbr_views, nbr_counts):
    score_scale = HEAD_DIM ** -0.5
    query_all = queries.reshape(VIEWS, TOK_VIEW, HEADS, HEAD_DIM)
    key_all = keys.reshape(VIEWS, TOK_VIEW, HEADS, HEAD_DIM)
    value_all = values.reshape(VIEWS, TOK_VIEW, HEADS, HEAD_DIM)
    grad_all = out_grad.reshape(VIEWS, TOK_VIEW, HEADS, HEAD_DIM)
    own_views = jnp.arange(VIEWS, dtype=jnp.int32)[:, None]
    block_views = jnp.concatenate([own_views, nbr_views.astype(jnp.int32)], axis=1)
    active_all = jnp.arange(1 + MAXNB, dtype=jnp.int32)[None, :] <= nbr_counts[:, None]

    def one_view(inputs):
        query_view, grad_view, picked, active = inputs
        key_block = key_all[picked].astype(jnp.float32)
        value_block = value_all[picked].astype(jnp.float32)
        query_wide = query_view.astype(jnp.float32)
        grad_wide = grad_view.astype(jnp.float32)
        scores = jnp.einsum("qhd,bkhd->hqbk", query_wide, key_block) * score_scale
        scores = jnp.where(active[None, None, :, None], scores, -jnp.inf)
        top = jnp.max(scores, axis=(2, 3), keepdims=True)
        expo = jnp.exp(scores - top)
        probs = expo / jnp.sum(expo, axis=(2, 3), keepdims=True)
        probs_low = probs.astype(jnp.bfloat16).astype(jnp.float32)
        attended = jnp.einsum("hqbk,bkhd->qhd", probs_low, value_block).astype(jnp.bfloat16)
        deltas = jnp.sum(grad_wide * attended.astype(jnp.float32), axis=2)
        dprobs = jnp.einsum("qhd,bkhd->hqbk", grad_wide, value_block)
        dscores = (probs * (dprobs - deltas.T[:, :, None, None])).astype(jnp.bfloat16).astype(jnp.float32)
        grad_query = (jnp.einsum("hqbk,bkhd->qhd", dscores, key_block) * score_scale).astype(jnp.bfloat16)
        key_terms = jnp.einsum("hqbk,qhd->bkhd", dscores, query_wide) * score_scale
        value_terms = jnp.einsum("hqbk,qhd->bkhd", probs_low, grad_wide)
        return attended, grad_query, key_terms, value_terms

    attended, grad_q, key_terms, value_terms = lax.map(one_view, (query_all, grad_all, block_views, active_all))
    flat_views = block_views.reshape(-1)
    total_key = jnp.zeros((VIEWS, TOK_VIEW, HEADS, HEAD_DIM), jnp.float32)
    total_key = total_key.at[flat_views].add(key_terms.reshape(-1, TOK_VIEW, HEADS, HEAD_DIM))
    total_value = jnp.zeros((VIEWS, TOK_VIEW, HEADS, HEAD_DIM), jnp.float32)
    total_value = total_value.at[flat_views].add(value_terms.reshape(-1, TOK_VIEW, HEADS, HEAD_DIM))
    shape_out = (VIEWS, TOK_VIEW, HEADS * HEAD_DIM)
    return (attended.reshape(shape_out), grad_q.reshape(shape_out),
            total_key.astype(jnp.bfloat16).reshape(shape_out), total_value.astype(jnp.bfloat16).reshape(shape_out))
```

```python
import functools

import jax
import jax.numpy as jnp
from jax import lax
from jax.experimental import pallas as pl
from jax.experimental.pallas import tpu as pltpu
from jax.sharding import Mesh, PartitionSpec as P

HEAD_DIM = 64
PAIR = 2 * HEAD_DIM
HEADS = 16
TOK = 768
PIECE = 192
ROW = 4
EDGE = 2
MAXNB = 3
SCALE = HEAD_DIM ** (-0.5)
BF = jnp.bfloat16
F32 = jnp.float32
VMEM_LIMIT = 60 * 1024 * 1024


def pack_kernel(a_ref, b_ref, out_ref):
    for h in range(out_ref.shape[0]):
        cols = slice(h * HEAD_DIM, (h + 1) * HEAD_DIM)
        out_ref[h] = jnp.concatenate([a_ref[:, cols], b_ref[:, cols]], axis=1)


def pack(a, b):
    steps = 4
    return pl.pallas_call(
        pack_kernel,
        grid=(steps,),
        in_specs=[pl.BlockSpec((PIECE, HEADS * HEAD_DIM // steps), lambda i: (0, i))] * 2,
        out_specs=pl.BlockSpec((HEADS // steps, PIECE, PAIR), lambda i: (i, 0, 0)),
        out_shape=jax.ShapeDtypeStruct((HEADS, PIECE, PAIR), BF),
    )(a, b)


def unpack_kernel(in_ref, a_ref, b_ref):
    for h in range(in_ref.shape[0]):
        cols = slice(h * HEAD_DIM, (h + 1) * HEAD_DIM)
        a_ref[:, cols] = in_ref[h, :, :HEAD_DIM]
        b_ref[:, cols] = in_ref[h, :, HEAD_DIM:]


def unpack(packed):
    steps = 4
    whole = jax.ShapeDtypeStruct((PIECE, HEADS * HEAD_DIM), BF)
    return pl.pallas_call(
        unpack_kernel,
        grid=(steps,),
        in_specs=[pl.BlockSpec((HEADS // steps, PIECE, PAIR), lambda i: (i, 0, 0))],
        out_specs=[pl.BlockSpec((PIECE, HEADS * HEAD_DIM // steps), lambda i: (0, i))] * 2,
        out_shape=[whole, whole],
    )(packed)


def dot(a, b):
    return jnp.dot(a, b, preferred_element_type=F32)


def attention_kernel(
    index_ref, count_ref, qg_ref, own_ref, edge_ref, mate_ref, mate_edge_ref,
    od_ref, dkv_ref,
    kv, kv_t, ones_v, total, expo, low, outs, tops, sem,
):
    copies = [
        pltpu.make_async_copy(own_ref, kv.at[0:ROW], sem.at[0]),
        pltpu.make_async_copy(edge_ref, kv.at[ROW : ROW + EDGE], sem.at[1]),
        pltpu.make_async_copy(mate_ref, kv.at[ROW + EDGE : 2 * ROW + EDGE], sem.at[2]),
        pltpu.make_async_copy(mate_edge_ref, kv.at[2 * ROW + EDGE : 2 * (ROW + EDGE)], sem.at[3]),
    ]
    for copy in copies:
        copy.start()
    for copy in copies:
        copy.wait()

    lane = lax.broadcasted_iota(jnp.int32, (TOK, PAIR), 1)
    sub = lax.broadcasted_iota(jnp.int32, (PAIR, TOK), 0)

    def prepare(i, carry):
        block = kv[i]
        kv_t[i, :PAIR, :] = block.T
        kv_t[i, PAIR:, :] = jnp.ones((16, TOK), BF)
        ones_v[i] = jnp.where(lane < HEAD_DIM, jnp.ones_like(block), block)
        total[i] = jnp.zeros((TOK, PAIR), F32)
        return carry

    lax.fori_loop(0, 2 * (ROW + EDGE), prepare, 0)

    def one_view(j, carry):
        qg = qg_ref[j]
        qg_t = qg.T
        q_t = jnp.where(sub < HEAD_DIM, qg_t * SCALE, jnp.zeros_like(qg_t)).astype(BF)
        used = 1 + count_ref[j]

        def forward(b, carry):
            top, acc = carry
            i = index_ref[j, b]
            scores = dot(kv[i], q_t)
            top_b = jnp.max(scores, axis=0, keepdims=True)
            e = jnp.exp(scores - top_b).astype(BF)
            expo[b] = e
            part = dot(kv_t[i, HEAD_DIM:, :], e)
            tops[b, :, :] = top_b
            new = jnp.maximum(top, top_b)
            acc = acc * jnp.exp(top - new) + part * jnp.exp(top_b - new)
            return new, acc

        top, acc = lax.fori_loop(
            0, used, forward,
            (jnp.full((1, TOK), -jnp.inf, F32), jnp.zeros((HEAD_DIM + 16, TOK), F32)),
        )
        inverse = 1.0 / acc[HEAD_DIM : HEAD_DIM + 1]
        att = acc[:HEAD_DIM] * inverse
        delta = jnp.sum(qg_t[HEAD_DIM:].astype(F32) * att, axis=0, keepdims=True)
        d_hi = delta.astype(BF)
        d_mid = (delta - d_hi.astype(F32)).astype(BF)
        d_lo = (delta - d_hi.astype(F32) - d_mid.astype(F32)).astype(BF)
        g_t = jnp.where(
            sub == 0, -d_hi,
            jnp.where(sub == 1, -d_mid,
                      jnp.where(sub == 2, -d_lo,
                                jnp.where(sub < HEAD_DIM, jnp.zeros_like(qg_t), qg_t))),
        )
        q_side = jnp.where(lane < HEAD_DIM, qg * SCALE, jnp.zeros_like(qg)).astype(BF)
        g_side = jnp.where(lane < HEAD_DIM, jnp.zeros_like(qg), qg)

        def backward(b, dq):
            i = index_ref[j, b]
            share = jnp.exp(tops[b] - top) * inverse
            dprobs = dot(ones_v[i], g_t)
            p = expo[b].astype(F32) * share
            ds = (p * dprobs).astype(BF)
            dq = dq + dot(kv_t[i, :HEAD_DIM, :], ds)
            total[i] += dot(ds, q_side) + dot(p.astype(BF), g_side)
            return dq

        dq = lax.fori_loop(0, used, backward, jnp.zeros((HEAD_DIM, TOK), F32))
        od = jnp.concatenate([att.astype(BF), (dq * SCALE).astype(BF)], axis=0)
        od_ref[j] = od.T
        return carry

    lax.fori_loop(0, ROW, one_view, 0)

    def emit(i, carry):
        dkv_ref[i] = total[i].astype(BF)
        return carry

    lax.fori_loop(0, 2 * (ROW + EDGE), emit, 0)


def attention(index, count, qg, own, edge, mate, mate_edge):
    window = 2 * (ROW + EDGE)
    hbm = pl.BlockSpec(memory_space=pl.ANY)
    smem = pl.BlockSpec(memory_space=pltpu.SMEM)
    vmem = pl.BlockSpec(memory_space=pltpu.VMEM)
    return pl.pallas_call(
        attention_kernel,
        in_specs=[smem, smem, vmem, hbm, hbm, hbm, hbm],
        out_specs=[vmem, vmem],
        out_shape=[
            jax.ShapeDtypeStruct((ROW, TOK, PAIR), BF),
            jax.ShapeDtypeStruct((window, TOK, PAIR), BF),
        ],
        scratch_shapes=[
            pltpu.VMEM((window, TOK, PAIR), BF),
            pltpu.VMEM((window, PAIR + 16, TOK), BF),
            pltpu.VMEM((window, TOK, PAIR), BF),
            pltpu.VMEM((window, TOK, PAIR), F32),
            pltpu.VMEM((1 + MAXNB, TOK, TOK), BF),
            pltpu.VMEM((TOK, 2 * TOK), BF),
            pltpu.VMEM((HEAD_DIM, TOK), F32),
            pltpu.VMEM((1 + MAXNB, 1, TOK), F32),
            pltpu.SemaphoreType.DMA((4,)),
        ],
        compiler_params=pltpu.CompilerParams(vmem_limit_bytes=VMEM_LIMIT),
    )(index, count, qg, own, edge, mate, mate_edge)


def block_index(nbr_views, nbr_counts):
    z, x, c = lax.axis_index("z"), lax.axis_index("x"), lax.axis_index("c")
    at = nbr_views[0] % (4 * ROW)
    same_row = (at // (2 * ROW)) == (z % 2)
    column = (at // 2) % ROW
    place = jnp.where(same_row, column, ROW + column % 2)
    place = jnp.where(at % 2 == c, place, place + ROW + EDGE)
    mine = jnp.concatenate([x[None].astype(jnp.int32), place, nbr_counts])
    everyone = lax.all_gather(mine, "x")
    return everyone[:, : 1 + MAXNB], everyone[:, 1 + MAXNB]


def local(queries, keys, values, out_grad, nbr_views, nbr_counts):
    index, count = block_index(nbr_views, nbr_counts)
    kv = pack(keys[0], values[0])
    qg = pack(queries[0], out_grad[0])
    own = lax.all_to_all(kv, ("x", "y"), 0, 0, tiled=True).reshape(ROW, TOK, PAIR)
    qg = lax.all_to_all(qg, ("x", "y"), 0, 0, tiled=True).reshape(ROW, TOK, PAIR)
    cores = [(0, 1), (1, 0)]
    rows = [(i, i ^ 1) for i in range(lax.axis_size("z"))]
    upper = lax.axis_index("z") % 2 == 1
    start = jnp.where(upper, 0, ROW - EDGE)
    edge = lax.ppermute(lax.dynamic_slice_in_dim(own, start, EDGE, 0), "z", rows)
    mate = lax.ppermute(own, "c", cores)
    mate_edge = lax.ppermute(edge, "c", cores)
    od, dkv = attention(index, count, qg, own, edge, mate, mate_edge)
    od = lax.all_to_all(od.reshape(HEADS, PIECE, PAIR), ("x", "y"), 0, 0, tiled=True)
    attended, grad_q = unpack(od)
    got = lax.ppermute(dkv[ROW + EDGE :], "c", cores)
    edge_sum = (dkv[ROW : ROW + EDGE].astype(F32) + got[ROW:].astype(F32)).astype(BF)
    edge_got = lax.ppermute(edge_sum, "z", rows)
    own_sum = dkv[:ROW].astype(F32) + got[:ROW].astype(F32)
    zero = jnp.zeros_like(edge_got)
    edge_full = jnp.concatenate(
        [jnp.where(upper, edge_got, zero), jnp.where(upper, zero, edge_got)], axis=0
    )
    dkv_sum = (own_sum + edge_full.astype(F32)).astype(BF)
    back = lax.all_to_all(dkv_sum.reshape(HEADS, PIECE, PAIR), ("x", "y"), 0, 0, tiled=True)
    grad_k, grad_v = unpack(back)
    return attended[None], grad_q[None], grad_k[None], grad_v[None]


def solution(mesh):
    fine = Mesh(mesh.devices.reshape(8, 4, 2, 4), ("z", "x", "c", "y"))
    views = ("z", "x", "c")
    tokens = P(views, "y", None)
    return jax.shard_map(
        local,
        mesh=fine,
        in_specs=(tokens, tokens, tokens, tokens, P(views, None), P(views)),
        out_specs=(tokens, tokens, tokens, tokens),
        check_vma=False,
    )
```

```python
import jax
import jax.numpy as jnp
from jax import lax
from jax.experimental import pallas as pl
from jax.experimental.pallas import tpu as pltpu
from jax.sharding import Mesh, PartitionSpec as P

HEAD_DIM = 64
PAIR = 2 * HEAD_DIM
HEADS = 16
WIDTH = HEADS * HEAD_DIM
TOK = 768
PIECE = 192
QUARTERS = TOK // PIECE
ROW = 4
EDGE = 2
NEAR = 2 * ROW
MAXNB = 3
SLOTS = 1 + MAXNB
SUMS = HEAD_DIM + 16
TOP = HEAD_DIM + 8
CODES = 32
NEAR_COUNT = CODES - 2
EDGE_COUNT = CODES - 1
KERNEL_MIB = 48
EDGE_MIB = 48
SCALE = HEAD_DIM ** (-0.5)
BF = jnp.bfloat16
F32 = jnp.float32

ANY = pl.BlockSpec(memory_space=pl.ANY)
HBM = pl.BlockSpec(memory_space=pltpu.HBM)
SMEM = pl.BlockSpec(memory_space=pltpu.SMEM)
VMEM = pl.BlockSpec(memory_space=pltpu.VMEM)


def params(mib):
    return pltpu.CompilerParams(vmem_limit_bytes=mib * 1024 * 1024)


def shape(dims, dtype=BF):
    return jax.ShapeDtypeStruct(dims, dtype)


def cost(flops, moved):
    return pl.CostEstimate(flops=flops, bytes_accessed=moved, transcendentals=0)


def block(*lead):
    return lead + (QUARTERS, PIECE, PAIR)


def pack_kernel(q_ref, k_ref, v_ref, g_ref, out_ref):
    for side, (a, b) in enumerate(((k_ref, v_ref), (q_ref, g_ref))):
        for h in range(HEADS):
            cols = slice(h * HEAD_DIM, (h + 1) * HEAD_DIM)
            out_ref[h, side] = jnp.concatenate([a[:, cols], b[:, cols]], axis=1)


def pack(*arrays):
    return pl.pallas_call(
        pack_kernel,
        in_specs=[VMEM] * 4,
        out_specs=VMEM,
        out_shape=shape((HEADS, 2, PIECE, PAIR)),
        compiler_params=params(60),
    )(*arrays)


def unpack_kernel(in_ref, a_ref, q_ref, k_ref, v_ref):
    for side, (a, b) in enumerate(((k_ref, v_ref), (a_ref, q_ref))):
        for h in range(HEADS):
            cols = slice(h * HEAD_DIM, (h + 1) * HEAD_DIM)
            a[:, cols] = in_ref[h, side, :, :HEAD_DIM]
            b[:, cols] = in_ref[h, side, :, HEAD_DIM:]


def unpack(packed):
    return pl.pallas_call(
        unpack_kernel,
        in_specs=[VMEM],
        out_specs=[VMEM] * 4,
        out_shape=[shape((PIECE, WIDTH))] * 4,
        compiler_params=params(16),
    )(packed)


def dot(a, b):
    return jnp.dot(a, b, preferred_element_type=F32)


def dot_nt(a, b):
    return lax.dot_general(a, b, (((1,), (1,)), ((), ())), preferred_element_type=F32)


def flat(ref):
    return ref[...].reshape(TOK, PAIR)


def low_lanes():
    return lax.broadcasted_iota(jnp.int32, (TOK, PAIR), 1) < HEAD_DIM


def query_side(qg):
    return jnp.where(low_lanes(), qg * SCALE, jnp.zeros_like(qg)).astype(BF)


def scores_of(kv, q_side):
    scores = dot_nt(kv, q_side)
    return scores, jnp.max(scores, axis=0, keepdims=True)


def values_of(kv, scores, top):
    e = jnp.exp(scores - top).astype(BF)
    left = jnp.concatenate([kv.T[HEAD_DIM:], jnp.ones((16, TOK), BF)], axis=0)
    part = dot(left, e)
    return e, jnp.concatenate([part[:TOP], jnp.broadcast_to(top, (8, TOK))], axis=0)


def grad_rows(qg_t, delta):
    d_hi = delta.astype(BF)
    rest = delta - d_hi.astype(F32)
    d_mid = rest.astype(BF)
    d_lo = (rest - d_mid.astype(F32)).astype(BF)
    sub = lax.broadcasted_iota(jnp.int32, (PAIR, TOK), 0)
    low = jnp.where(sub == 0, -d_hi, jnp.where(sub == 1, -d_mid, jnp.where(sub == 2, -d_lo, jnp.zeros_like(qg_t))))
    return jnp.where(sub < HEAD_DIM, low, qg_t)


def backward_pair(kv, e, share, g_t, q_side, g_side):
    dprobs = dot(jnp.where(low_lanes(), jnp.ones_like(kv), kv), g_t)
    p = e.astype(F32) * share
    ds = (p * dprobs).astype(BF)
    dq = dot(kv.T[:HEAD_DIM], ds)
    return dq, dot(ds, q_side) + dot(p.astype(BF), g_side)


def decode(codes, n):
    code = codes[n]
    return code >> 6, (code >> 4) & 3, code & 15


def list_pairs(x, rows, codes):
    n = jnp.int32(0)
    for kind in range(2):
        for t in range(ROW):
            view = (x + t) & (ROW - 1)
            for b in range(SLOTS):
                place = rows[t, b]
                codes[n] = view * 64 + b * 16 + place
                wanted = place < NEAR if kind == 0 else place >= NEAR
                n = n + jnp.where(jnp.logical_and(b < rows[t, SLOTS], wanted), 1, 0)
        if kind == 0:
            near = n
    codes[NEAR_COUNT] = near
    codes[EDGE_COUNT] = n - near


def merge(acc, j, part, top):
    old_top = acc[j, TOP : TOP + 1]
    new_top = jnp.maximum(old_top, top)
    acc[j, :TOP] = acc[j, :TOP] * jnp.exp(old_top - new_top) + part[:TOP] * jnp.exp(top - new_top)
    acc[j, TOP:] = jnp.broadcast_to(new_top, (8, TOK))


def forward_near_kernel(
    x_ref, rows, arrived, mate, e_out, acc_out, tops_out, codes,
    kv, qg, q_side, scores, top_now, e, acc, tops, sems, e_sems, out_sems,
):
    loads = []
    for x in range(ROW):
        loads.append(pltpu.make_async_copy(arrived.at[x, :, 1], qg.at[x], sems.at[x]))
        loads.append(pltpu.make_async_copy(arrived.at[x, :, 0], kv.at[x], sems.at[ROW + x]))
    loads.append(pltpu.make_async_copy(mate, kv.at[ROW:NEAR], sems.at[2 * ROW]))
    for load in loads:
        load.start()
    list_pairs(x_ref[0], rows, codes)
    acc[...] = jnp.zeros_like(acc)
    for x in range(ROW):
        acc[x, TOP:] = jnp.full((8, TOK), -jnp.inf, F32)
    for load in loads:
        load.wait()
    for x in range(ROW):
        q_side[x] = query_side(flat(qg.at[x]))

    def store(j, b, ring):
        return pltpu.make_async_copy(e.at[ring], e_out.at[j, b], e_sems.at[ring])

    def score(n, ring):
        j, _, i = decode(codes, n)
        scores[ring], top_now[ring] = scores_of(flat(kv.at[i]), q_side[j])

    count = codes[NEAR_COUNT]
    score(0, 0)

    def one_pair(n, carry):
        ring = n % 2
        j, b, i = decode(codes, n)

        @pl.when(n >= 2)
        def _():
            store(j, b, ring).wait()

        top = top_now[ring]
        e[ring], part = values_of(flat(kv.at[i]), scores[ring], top)
        score(jnp.minimum(n + 1, count - 1), 1 - ring)
        merge(acc, j, part, top)
        tops[j, pl.ds(b, 1), :] = top
        store(j, b, ring).start()
        return carry

    lax.fori_loop(0, count, one_pair, 0)
    outs = [
        pltpu.make_async_copy(acc, acc_out, out_sems.at[0]),
        pltpu.make_async_copy(tops, tops_out, out_sems.at[1]),
    ]
    for out in outs:
        out.start()
    for ring in range(2):
        store(0, 0, ring).wait()
    for out in outs:
        out.wait()


def forward_near(x, rows, arrived, mate):
    return pl.pallas_call(
        forward_near_kernel,
        in_specs=[SMEM] * 2 + [ANY] * 2,
        out_specs=[HBM, ANY, ANY, SMEM],
        out_shape=[
            shape((ROW, SLOTS, TOK, TOK)),
            shape((ROW, SUMS, TOK), F32),
            shape((ROW, 8, TOK), F32),
            shape((CODES,), jnp.int32),
        ],
        scratch_shapes=[
            pltpu.VMEM(block(NEAR), BF),
            pltpu.VMEM(block(ROW), BF),
            pltpu.VMEM((ROW, TOK, PAIR), BF),
            pltpu.VMEM((2, TOK, TOK), F32),
            pltpu.VMEM((2, 1, TOK), F32),
            pltpu.VMEM((2, TOK, TOK), BF),
            pltpu.VMEM((ROW, SUMS, TOK), F32),
            pltpu.VMEM((ROW, 8, TOK), F32),
            pltpu.SemaphoreType.DMA((2 * ROW + 1,)),
            pltpu.SemaphoreType.DMA((2,)),
            pltpu.SemaphoreType.DMA((2,)),
        ],
        compiler_params=params(KERNEL_MIB),
        cost_estimate=cost(9 * 10**9, 20 * 10**6),
    )(x, rows, arrived, mate)


def edge_kernel(
    codes, arrived, edge, mate_edge, acc_in, tops_in,
    att_out, dq_out, shares_out, g_t_out, d_edge, d_mate_edge,
    kv, qg, acc, tops, e, scores, top_now, total, dq_sum, q_side, g_side, g_t, att, shares, d_out, sems, out_sems,
):
    loads = []
    for x in range(ROW):
        loads.append(pltpu.make_async_copy(arrived.at[x, :, 1], qg.at[x], sems.at[x]))
    loads.append(pltpu.make_async_copy(edge, kv.at[0:EDGE], sems.at[ROW]))
    loads.append(pltpu.make_async_copy(mate_edge, kv.at[EDGE : 2 * EDGE], sems.at[ROW + 1]))
    loads.append(pltpu.make_async_copy(acc_in, acc, sems.at[ROW + 2]))
    loads.append(pltpu.make_async_copy(tops_in, tops, sems.at[ROW + 3]))
    for load in loads:
        load.start()
    total[...] = jnp.zeros_like(total)
    dq_sum[...] = jnp.zeros_like(dq_sum)
    for load in loads:
        load.wait()
    for x in range(ROW):
        qg_now = flat(qg.at[x])
        q_side[x] = query_side(qg_now)
        g_side[x] = jnp.where(low_lanes(), jnp.zeros_like(qg_now), qg_now)

    first, count = codes[NEAR_COUNT], codes[EDGE_COUNT]

    def score(n, ring):
        j, _, i = decode(codes, first + n)
        scores[ring], top_now[ring] = scores_of(flat(kv.at[i - NEAR]), q_side[j])

    @pl.when(count > 0)
    def _():
        score(0, 0)

    def one_forward(n, carry):
        ring = n % 2
        j, b, i = decode(codes, first + n)
        top = top_now[ring]
        e[n], part = values_of(flat(kv.at[i - NEAR]), scores[ring], top)
        score(jnp.minimum(n + 1, count - 1), 1 - ring)
        merge(acc, j, part, top)
        tops[j, pl.ds(b, 1), :] = top
        return carry

    lax.fori_loop(0, count, one_forward, 0)

    for j in range(ROW):
        inverse = 1.0 / acc[j, HEAD_DIM : HEAD_DIM + 1]
        att_now = acc[j, :HEAD_DIM] * inverse
        qg_t = flat(qg.at[j]).T
        delta = jnp.sum(qg_t[HEAD_DIM:].astype(F32) * att_now, axis=0, keepdims=True)
        att[j] = att_now.astype(BF)
        shares[j] = jnp.exp(tops[j] - acc[j, TOP : TOP + 1]) * inverse
        g_t[j] = grad_rows(qg_t, delta)

    early = [
        pltpu.make_async_copy(att, att_out, out_sems.at[0]),
        pltpu.make_async_copy(shares, shares_out, out_sems.at[1]),
        pltpu.make_async_copy(g_t, g_t_out, out_sems.at[2]),
    ]
    for out in early:
        out.start()

    def one_backward(n, carry):
        j, b, i = decode(codes, first + n)
        share = shares[j, pl.ds(b, 1), :]
        dq, terms = backward_pair(flat(kv.at[i - NEAR]), e[n], share, g_t[j], q_side[j], g_side[j])
        total[i - NEAR] += terms
        dq_sum[j] += dq
        return carry

    lax.fori_loop(0, count, one_backward, 0)
    for i in range(2 * EDGE):
        d_out[i] = total[i].astype(BF).reshape(QUARTERS, PIECE, PAIR)
    late = [
        pltpu.make_async_copy(d_out.at[0:EDGE], d_edge, out_sems.at[3]),
        pltpu.make_async_copy(d_out.at[EDGE : 2 * EDGE], d_mate_edge, out_sems.at[4]),
        pltpu.make_async_copy(dq_sum, dq_out, out_sems.at[5]),
    ]
    for out in late:
        out.start()
    for out in early + late:
        out.wait()


def edges(codes, arrived, edge, mate_edge, acc, tops):
    return pl.pallas_call(
        edge_kernel,
        in_specs=[SMEM] + [ANY] * 5,
        out_specs=[ANY] * 6,
        out_shape=[
            shape((ROW, HEAD_DIM, TOK)),
            shape((ROW, HEAD_DIM, TOK), F32),
            shape((ROW, 8, TOK), F32),
            shape((ROW, PAIR, TOK)),
            shape(block(EDGE)),
            shape(block(EDGE)),
        ],
        scratch_shapes=[
            pltpu.VMEM(block(2 * EDGE), BF),
            pltpu.VMEM(block(ROW), BF),
            pltpu.VMEM((ROW, SUMS, TOK), F32),
            pltpu.VMEM((ROW, 8, TOK), F32),
            pltpu.VMEM((ROW * MAXNB, TOK, TOK), BF),
            pltpu.VMEM((2, TOK, TOK), F32),
            pltpu.VMEM((2, 1, TOK), F32),
            pltpu.VMEM((2 * EDGE, TOK, PAIR), F32),
            pltpu.VMEM((ROW, HEAD_DIM, TOK), F32),
            pltpu.VMEM((ROW, TOK, PAIR), BF),
            pltpu.VMEM((ROW, TOK, PAIR), BF),
            pltpu.VMEM((ROW, PAIR, TOK), BF),
            pltpu.VMEM((ROW, HEAD_DIM, TOK), BF),
            pltpu.VMEM((ROW, 8, TOK), F32),
            pltpu.VMEM(block(2 * EDGE), BF),
            pltpu.SemaphoreType.DMA((ROW + 4,)),
            pltpu.SemaphoreType.DMA((6,)),
        ],
        compiler_params=params(EDGE_MIB),
        cost_estimate=cost(9 * 10**9, 10 * 10**6),
    )(codes, arrived, edge, mate_edge, acc, tops)


def backward_near_kernel(
    codes, arrived, mate, e_in, att_in, dq_in, shares_in, g_t_in, edge_sum,
    od_out, d_own, d_mate,
    kv, qg, e, total, dq_sum, q_side, g_side, g_t, att, shares, od, d_out, sems, e_sems, out_sems,
):
    loads = []
    for x in range(ROW):
        loads.append(pltpu.make_async_copy(arrived.at[x, :, 1], qg.at[x], sems.at[x]))
        loads.append(pltpu.make_async_copy(arrived.at[x, :, 0], kv.at[x], sems.at[ROW + x]))
    loads.append(pltpu.make_async_copy(mate, kv.at[ROW:NEAR], sems.at[2 * ROW]))
    loads.append(pltpu.make_async_copy(g_t_in, g_t, sems.at[2 * ROW + 1]))
    loads.append(pltpu.make_async_copy(shares_in, shares, sems.at[2 * ROW + 2]))
    later = [
        pltpu.make_async_copy(dq_in, dq_sum, sems.at[2 * ROW + 3]),
        pltpu.make_async_copy(att_in, att, sems.at[2 * ROW + 4]),
    ]

    def fetch(n, ring):
        j, b, _ = decode(codes, n)
        return pltpu.make_async_copy(e_in.at[j, b], e.at[ring], e_sems.at[ring])

    count = codes[NEAR_COUNT]
    fetch(0, 0).start()
    for load in loads + later:
        load.start()
    total[...] = jnp.zeros_like(total)
    for load in loads:
        load.wait()
    for x in range(ROW):
        qg_now = flat(qg.at[x])
        q_side[x] = query_side(qg_now)
        g_side[x] = jnp.where(low_lanes(), jnp.zeros_like(qg_now), qg_now)
    for load in later:
        load.wait()

    def one_pair(n, carry):
        ring = n % 2
        j, b, i = decode(codes, n)
        fetch(n, ring).wait()

        @pl.when(n + 1 < count)
        def _():
            fetch(n + 1, 1 - ring).start()

        share = shares[j, pl.ds(b, 1), :]
        dq, terms = backward_pair(flat(kv.at[i]), e[ring], share, g_t[j], q_side[j], g_side[j])
        total[i] += terms
        dq_sum[j] += dq
        return carry

    lax.fori_loop(0, count, one_pair, 0)
    outs = [
        pltpu.make_async_copy(d_out.at[ROW:NEAR], d_mate, out_sems.at[ROW]),
        pltpu.make_async_copy(d_out.at[0:ROW], d_own, out_sems.at[ROW + 1]),
    ]
    for x in range(ROW):
        outs.append(pltpu.make_async_copy(od.at[x], od_out.at[x], out_sems.at[x]))
    for i in range(ROW):
        d_out[ROW + i] = total[ROW + i].astype(BF).reshape(QUARTERS, PIECE, PAIR)
    outs[0].start()
    for i in range(ROW):
        d_out[i] = total[i].astype(BF).reshape(QUARTERS, PIECE, PAIR)
    outs[1].start()
    for x in range(ROW):
        both = jnp.concatenate([att[x], (dq_sum[x] * SCALE).astype(BF)], axis=0)
        od[x] = both.T.reshape(QUARTERS, PIECE, PAIR)
        outs[2 + x].start()
    for store in outs:
        store.wait()


def backward_near(codes, arrived, mate, e, att, dq, shares, g_t, edge_sum):
    return pl.pallas_call(
        backward_near_kernel,
        in_specs=[SMEM, ANY, ANY, HBM] + [ANY] * 5,
        out_specs=[ANY] * 3,
        out_shape=[shape(block(ROW))] * 3,
        scratch_shapes=[
            pltpu.VMEM(block(NEAR), BF),
            pltpu.VMEM(block(ROW), BF),
            pltpu.VMEM((2, TOK, TOK), BF),
            pltpu.VMEM((NEAR, TOK, PAIR), F32),
            pltpu.VMEM((ROW, HEAD_DIM, TOK), F32),
            pltpu.VMEM((ROW, TOK, PAIR), BF),
            pltpu.VMEM((ROW, TOK, PAIR), BF),
            pltpu.VMEM((ROW, PAIR, TOK), BF),
            pltpu.VMEM((ROW, HEAD_DIM, TOK), BF),
            pltpu.VMEM((ROW, 8, TOK), F32),
            pltpu.VMEM(block(ROW), BF),
            pltpu.VMEM(block(NEAR), BF),
            pltpu.SemaphoreType.DMA((2 * ROW + 5,)),
            pltpu.SemaphoreType.DMA((2,)),
            pltpu.SemaphoreType.DMA((ROW + 2,)),
        ],
        compiler_params=params(KERNEL_MIB),
        cost_estimate=cost(15 * 10**9, 20 * 10**6),
    )(codes, arrived, mate, e, att, dq, shares, g_t, edge_sum)


def fold_kernel(upper, own, got, edge_got, od, out, sums, sems, od_sem):
    kept = pltpu.make_async_copy(od, out.at[:, :, 1], od_sem)
    kept.start()
    stores = []
    for x in range(ROW):
        total = own[x].astype(F32) + got[x].astype(F32)
        listed = upper[0] == (0 if x >= EDGE else 1)
        far = edge_got[x % EDGE].astype(F32)
        sums[x] = (total + jnp.where(listed, far, jnp.zeros_like(far))).astype(BF)
        stores.append(pltpu.make_async_copy(sums.at[x], out.at[x, :, 0], sems.at[x]))
        stores[x].start()
    for store in stores:
        store.wait()
    kept.wait()


def fold(upper, own, got, edge_got, od):
    return pl.pallas_call(
        fold_kernel,
        in_specs=[SMEM, VMEM, VMEM, VMEM, ANY],
        out_specs=HBM,
        out_shape=shape((ROW, QUARTERS, 2, PIECE, PAIR)),
        scratch_shapes=[
            pltpu.VMEM(block(ROW), BF),
            pltpu.SemaphoreType.DMA((ROW,)),
            pltpu.SemaphoreType.DMA,
        ],
        compiler_params=params(16),
    )(upper, own, got, edge_got, od)


def block_rows(nbr_views, nbr_counts):
    z, x, c = lax.axis_index("z"), lax.axis_index("x"), lax.axis_index("c")
    at = nbr_views[0] % (4 * ROW)
    same_row = (at // NEAR) == (z % 2)
    column = (at // 2) % ROW
    place = jnp.where(same_row, column, NEAR + column % EDGE)
    place = place + jnp.where(at % 2 == c, 0, jnp.where(same_row, ROW, EDGE))
    mine = jnp.concatenate([x[None].astype(jnp.int32), place, nbr_counts + 1]).astype(jnp.int32)
    rows = [mine]
    for by in range(1, ROW):
        rows.append(lax.ppermute(mine, "x", [(i, (i - by) % ROW) for i in range(ROW)]))
    return x[None].astype(jnp.int32), jnp.stack(rows)


def local(queries, keys, values, out_grad, nbr_views, nbr_counts):
    x, rows_of_views = block_rows(nbr_views, nbr_counts)
    cores = [(0, 1), (1, 0)]
    rows = [(i, i ^ 1) for i in range(lax.axis_size("z"))]
    upper = lax.axis_index("z") % 2
    packed = pack(queries[0], keys[0], values[0], out_grad[0])
    arrived = lax.all_to_all(packed.reshape(HEADS, 2 * PIECE, PAIR), ("x", "y"), 0, 0, tiled=True)
    arrived, rows_of_views = lax.optimization_barrier((arrived, rows_of_views))
    arrived = arrived.reshape(ROW, QUARTERS, 2, PIECE, PAIR)
    start = jnp.where(upper == 1, 0, ROW - EDGE)
    edge = lax.ppermute(lax.dynamic_slice_in_dim(arrived, start, EDGE, 0)[:, :, 0], "z", rows)
    mate = lax.ppermute(arrived[:, :, 0], "c", cores)
    e, acc, tops, codes = forward_near(x, rows_of_views, arrived, mate)
    edge, acc = lax.optimization_barrier((edge, acc))
    mate_edge = lax.ppermute(edge, "c", cores)
    att, dq, shares, g_t, d_edge, d_mate_edge = edges(codes, arrived, edge, mate_edge, acc, tops)
    edge_sum = d_edge.astype(F32) + lax.ppermute(d_mate_edge, "c", cores).astype(F32)
    edge_sum = edge_sum.astype(BF)
    edge_got = lax.ppermute(edge_sum, "z", rows)
    od, d_own, d_mate = backward_near(codes, arrived, mate, e, att, dq, shares, g_t, edge_sum)
    d_mate, edge_got = lax.optimization_barrier((d_mate, edge_got))
    got = lax.ppermute(d_mate, "c", cores)
    out = fold(upper.astype(jnp.int32)[None], d_own, got, edge_got, od)
    back = lax.all_to_all(out.reshape(HEADS, 2 * PIECE, PAIR), ("x", "y"), 0, 0, tiled=True)
    results = unpack(back.reshape(HEADS, 2, PIECE, PAIR))
    return tuple(result[None] for result in results)


def solution(mesh):
    fine = Mesh(mesh.devices.reshape(8, 4, 2, 4), ("z", "x", "c", "y"))
    views = ("z", "x", "c")
    tokens = P(views, "y", None)
    return jax.shard_map(
        local,
        mesh=fine,
        in_specs=(tokens, tokens, tokens, tokens, P(views, None), P(views)),
        out_specs=(tokens, tokens, tokens, tokens),
        check_vma=False,
    )
```

```python
import jax
import jax.numpy as jnp
from jax import lax
from jax.experimental import pallas as pl
from jax.experimental.pallas import tpu as pltpu
from jax.sharding import Mesh, PartitionSpec as P

HEAD_DIM = 64
PAIR = 2 * HEAD_DIM
HEADS = 16
WIDTH = HEADS * HEAD_DIM
TOK = 768
PIECE = 192
QUARTERS = TOK // PIECE
ROW = 4
EDGE = 2
NEAR = 2 * ROW
MAXNB = 3
SLOTS = 1 + MAXNB
SUMS = HEAD_DIM + 16
TOP = HEAD_DIM + 8
CODES = 32
NEAR_COUNT = CODES - 2
EDGE_COUNT = CODES - 1
KERNEL_MIB = 48
EDGE_MIB = 48
SCALE = HEAD_DIM ** (-0.5)
BF = jnp.bfloat16
F32 = jnp.float32

ANY = pl.BlockSpec(memory_space=pl.ANY)
HBM = pl.BlockSpec(memory_space=pltpu.HBM)
SMEM = pl.BlockSpec(memory_space=pltpu.SMEM)
VMEM = pl.BlockSpec(memory_space=pltpu.VMEM)


def params(mib):
    return pltpu.CompilerParams(vmem_limit_bytes=mib * 1024 * 1024)


def shape(dims, dtype=BF):
    return jax.ShapeDtypeStruct(dims, dtype)


def cost(flops, moved):
    return pl.CostEstimate(flops=flops, bytes_accessed=moved, transcendentals=0)


def block(*lead):
    return lead + (QUARTERS, PIECE, PAIR)


def pack_kernel(q_ref, k_ref, v_ref, g_ref, out_ref):
    for side, (a, b) in enumerate(((k_ref, v_ref), (q_ref, g_ref))):
        for h in range(HEADS):
            cols = slice(h * HEAD_DIM, (h + 1) * HEAD_DIM)
            out_ref[h, side] = jnp.concatenate([a[:, cols], b[:, cols]], axis=1)


def pack(*arrays):
    steps = 2
    return pl.pallas_call(
        pack_kernel,
        grid=(steps,),
        in_specs=[pl.BlockSpec((PIECE // steps, WIDTH), lambda i: (i, 0))] * 4,
        out_specs=pl.BlockSpec((HEADS, 2, PIECE // steps, PAIR), lambda i: (0, 0, i, 0)),
        out_shape=shape((HEADS, 2, PIECE, PAIR)),
        compiler_params=params(60),
    )(*arrays)


def unpack_kernel(in_ref, a_ref, q_ref, k_ref, v_ref, a, q, k, v, sems):
    stores = []
    for side, pairs in enumerate((((k, k_ref), (v, v_ref)), ((a, a_ref), (q, q_ref)))):
        for h in range(HEADS):
            cols = slice(h * HEAD_DIM, (h + 1) * HEAD_DIM)
            pairs[0][0][:, cols] = in_ref[h, side, :, :HEAD_DIM]
            pairs[1][0][:, cols] = in_ref[h, side, :, HEAD_DIM:]
        for scratch, out in pairs:
            stores.append(pltpu.make_async_copy(scratch, out, sems.at[len(stores)]))
            stores[-1].start()
    for store in stores:
        store.wait()


def unpack(packed):
    return pl.pallas_call(
        unpack_kernel,
        in_specs=[VMEM],
        out_specs=[HBM] * 4,
        out_shape=[shape((PIECE, WIDTH))] * 4,
        scratch_shapes=[pltpu.VMEM((PIECE, WIDTH), BF)] * 4 + [pltpu.SemaphoreType.DMA((4,))],
        compiler_params=params(16),
    )(packed)


def dot(a, b):
    return jnp.dot(a, b, preferred_element_type=F32)


def dot_nt(a, b):
    return lax.dot_general(a, b, (((1,), (1,)), ((), ())), preferred_element_type=F32)


def flat(ref):
    return ref[...].reshape(TOK, PAIR)


def low_lanes():
    return lax.broadcasted_iota(jnp.int32, (TOK, PAIR), 1) < HEAD_DIM


def query_side(qg):
    return jnp.where(low_lanes(), qg * SCALE, jnp.zeros_like(qg)).astype(BF)


def scores_of(kv, q_side):
    scores = dot_nt(kv, q_side)
    return scores, jnp.max(scores, axis=0, keepdims=True)


def values_of(kv, scores, top):
    e = jnp.exp(scores - top).astype(BF)
    left = jnp.concatenate([kv.T[HEAD_DIM:], jnp.ones((16, TOK), BF)], axis=0)
    part = dot(left, e)
    return e, jnp.concatenate([part[:TOP], jnp.broadcast_to(top, (8, TOK))], axis=0)


def grad_rows(qg_t, delta):
    d_hi = delta.astype(BF)
    rest = delta - d_hi.astype(F32)
    d_mid = rest.astype(BF)
    d_lo = (rest - d_mid.astype(F32)).astype(BF)
    sub = lax.broadcasted_iota(jnp.int32, (PAIR, TOK), 0)
    low = jnp.where(sub == 0, -d_hi, jnp.where(sub == 1, -d_mid, jnp.where(sub == 2, -d_lo, jnp.zeros_like(qg_t))))
    return jnp.where(sub < HEAD_DIM, low, qg_t)


def backward_pair(kv, e, share, g_t, q_side, g_side):
    dprobs = dot(jnp.where(low_lanes(), jnp.ones_like(kv), kv), g_t)
    p = e.astype(F32) * share
    ds = (p * dprobs).astype(BF)
    dq = dot(kv.T[:HEAD_DIM], ds)
    return dq, dot(jnp.concatenate([ds, p.astype(BF)], axis=1), jnp.concatenate([q_side, g_side], axis=0))


def decode(codes, n):
    code = codes[n]
    return code >> 6, (code >> 4) & 3, code & 15


def list_pairs(x, rows, codes):
    n = jnp.int32(0)
    for kind in range(2):
        for t in range(ROW):
            view = (x + t) & (ROW - 1)
            for b in range(SLOTS):
                place = rows[t, b]
                codes[n] = view * 64 + b * 16 + place
                wanted = place < NEAR if kind == 0 else place >= NEAR
                n = n + jnp.where(jnp.logical_and(b < rows[t, SLOTS], wanted), 1, 0)
        if kind == 0:
            near = n
    codes[NEAR_COUNT] = near
    codes[EDGE_COUNT] = n - near


def merge(acc, j, part, top):
    old_top = acc[j, TOP : TOP + 1]
    new_top = jnp.maximum(old_top, top)
    acc[j, :TOP] = acc[j, :TOP] * jnp.exp(old_top - new_top) + part[:TOP] * jnp.exp(top - new_top)
    acc[j, TOP:] = jnp.broadcast_to(new_top, (8, TOK))


def forward_near_kernel(
    x_ref, rows, arrived, mate, e_out, acc_out, tops_out, codes,
    kv, qg, q_side, scores, top_now, e, acc, tops, sems, e_sems, out_sems,
):
    loads = [
        pltpu.make_async_copy(arrived.at[:, :, 1], qg, sems.at[0]),
        pltpu.make_async_copy(arrived.at[:, :, 0], kv.at[0:ROW], sems.at[1]),
        pltpu.make_async_copy(mate, kv.at[ROW:NEAR], sems.at[2]),
    ]
    for load in loads:
        load.start()
    list_pairs(x_ref[0], rows, codes)
    acc[...] = jnp.zeros_like(acc)
    for x in range(ROW):
        acc[x, TOP:] = jnp.full((8, TOK), -jnp.inf, F32)
    for load in loads:
        load.wait()
    for x in range(ROW):
        q_side[x] = query_side(flat(qg.at[x]))

    def store(j, b, ring):
        return pltpu.make_async_copy(e.at[ring], e_out.at[j, b], e_sems.at[ring])

    def score(n, ring):
        j, _, i = decode(codes, n)
        scores[ring], top_now[ring] = scores_of(flat(kv.at[i]), q_side[j])

    count = codes[NEAR_COUNT]
    score(0, 0)

    def one_pair(n, carry):
        ring = n % 2
        j, b, i = decode(codes, n)

        @pl.when(n >= 2)
        def _():
            store(j, b, ring).wait()

        top = top_now[ring]
        e[ring], part = values_of(flat(kv.at[i]), scores[ring], top)
        score(jnp.minimum(n + 1, count - 1), 1 - ring)
        merge(acc, j, part, top)
        tops[j, pl.ds(b, 1), :] = top
        store(j, b, ring).start()
        return carry

    lax.fori_loop(0, count, one_pair, 0)
    outs = [
        pltpu.make_async_copy(acc, acc_out, out_sems.at[0]),
        pltpu.make_async_copy(tops, tops_out, out_sems.at[1]),
    ]
    for out in outs:
        out.start()
    for ring in range(2):
        store(0, 0, ring).wait()
    for out in outs:
        out.wait()


def forward_near(x, rows, arrived, mate):
    return pl.pallas_call(
        forward_near_kernel,
        in_specs=[SMEM] * 2 + [ANY] * 2,
        out_specs=[HBM, ANY, ANY, SMEM],
        out_shape=[
            shape((ROW, SLOTS, TOK, TOK)),
            shape((ROW, SUMS, TOK), F32),
            shape((ROW, 8, TOK), F32),
            shape((CODES,), jnp.int32),
        ],
        scratch_shapes=[
            pltpu.VMEM(block(NEAR), BF),
            pltpu.VMEM(block(ROW), BF),
            pltpu.VMEM((ROW, TOK, PAIR), BF),
            pltpu.VMEM((2, TOK, TOK), F32),
            pltpu.VMEM((2, 1, TOK), F32),
            pltpu.VMEM((2, TOK, TOK), BF),
            pltpu.VMEM((ROW, SUMS, TOK), F32),
            pltpu.VMEM((ROW, 8, TOK), F32),
            pltpu.SemaphoreType.DMA((2 * ROW + 1,)),
            pltpu.SemaphoreType.DMA((2,)),
            pltpu.SemaphoreType.DMA((2,)),
        ],
        compiler_params=params(KERNEL_MIB),
        cost_estimate=cost(9 * 10**9, 20 * 10**6),
    )(x, rows, arrived, mate)


def edge_kernel(
    codes, arrived, edge, mate_edge, acc_in, tops_in,
    att_out, dq_out, shares_out, g_t_out, d_edge, d_mate_edge,
    kv, qg, acc, tops, e, scores, top_now, total, dq_sum, q_side, g_side, g_t, att, shares, d_out, sems, out_sems,
):
    loads = [pltpu.make_async_copy(arrived.at[:, :, 1], qg, sems.at[0])]
    loads.append(pltpu.make_async_copy(edge, kv.at[0:EDGE], sems.at[ROW]))
    loads.append(pltpu.make_async_copy(mate_edge, kv.at[EDGE : 2 * EDGE], sems.at[ROW + 1]))
    loads.append(pltpu.make_async_copy(acc_in, acc, sems.at[ROW + 2]))
    loads.append(pltpu.make_async_copy(tops_in, tops, sems.at[ROW + 3]))
    for load in loads:
        load.start()
    total[...] = jnp.zeros_like(total)
    dq_sum[...] = jnp.zeros_like(dq_sum)
    for load in loads:
        load.wait()
    for x in range(ROW):
        qg_now = flat(qg.at[x])
        q_side[x] = query_side(qg_now)
        g_side[x] = jnp.where(low_lanes(), jnp.zeros_like(qg_now), qg_now)

    first, count = codes[NEAR_COUNT], codes[EDGE_COUNT]

    def score(n, ring):
        j, _, i = decode(codes, first + n)
        scores[ring], top_now[ring] = scores_of(flat(kv.at[i - NEAR]), q_side[j])

    @pl.when(count > 0)
    def _():
        score(0, 0)

    def one_forward(n, carry):
        ring = n % 2
        j, b, i = decode(codes, first + n)
        top = top_now[ring]
        e[n], part = values_of(flat(kv.at[i - NEAR]), scores[ring], top)
        score(jnp.minimum(n + 1, count - 1), 1 - ring)
        merge(acc, j, part, top)
        tops[j, pl.ds(b, 1), :] = top
        return carry

    lax.fori_loop(0, count, one_forward, 0)

    for j in range(ROW):
        inverse = 1.0 / acc[j, HEAD_DIM : HEAD_DIM + 1]
        att_now = acc[j, :HEAD_DIM] * inverse
        qg_t = flat(qg.at[j]).T
        delta = jnp.sum(qg_t[HEAD_DIM:].astype(F32) * att_now, axis=0, keepdims=True)
        att[j] = att_now.astype(BF)
        shares[j] = jnp.exp(tops[j] - acc[j, TOP : TOP + 1]) * inverse
        g_t[j] = grad_rows(qg_t, delta)

    early = [
        pltpu.make_async_copy(att, att_out, out_sems.at[0]),
        pltpu.make_async_copy(shares, shares_out, out_sems.at[1]),
        pltpu.make_async_copy(g_t, g_t_out, out_sems.at[2]),
    ]
    for out in early:
        out.start()

    def one_backward(n, carry):
        j, b, i = decode(codes, first + n)
        share = shares[j, pl.ds(b, 1), :]
        dq, terms = backward_pair(flat(kv.at[i - NEAR]), e[n], share, g_t[j], q_side[j], g_side[j])
        total[i - NEAR] += terms
        dq_sum[j] += dq
        return carry

    lax.fori_loop(0, count, one_backward, 0)
    for i in range(2 * EDGE):
        d_out[i] = total[i].astype(BF).reshape(QUARTERS, PIECE, PAIR)
    late = [
        pltpu.make_async_copy(d_out.at[0:EDGE], d_edge, out_sems.at[3]),
        pltpu.make_async_copy(d_out.at[EDGE : 2 * EDGE], d_mate_edge, out_sems.at[4]),
        pltpu.make_async_copy(dq_sum, dq_out, out_sems.at[5]),
    ]
    for out in late:
        out.start()
    for out in early + late:
        out.wait()


def edges(codes, arrived, edge, mate_edge, acc, tops):
    return pl.pallas_call(
        edge_kernel,
        in_specs=[SMEM] + [ANY] * 5,
        out_specs=[ANY] * 6,
        out_shape=[
            shape((ROW, HEAD_DIM, TOK)),
            shape((ROW, HEAD_DIM, TOK), F32),
            shape((ROW, 8, TOK), F32),
            shape((ROW, PAIR, TOK)),
            shape(block(EDGE)),
            shape(block(EDGE)),
        ],
        scratch_shapes=[
            pltpu.VMEM(block(2 * EDGE), BF),
            pltpu.VMEM(block(ROW), BF),
            pltpu.VMEM((ROW, SUMS, TOK), F32),
            pltpu.VMEM((ROW, 8, TOK), F32),
            pltpu.VMEM((ROW * MAXNB, TOK, TOK), BF),
            pltpu.VMEM((2, TOK, TOK), F32),
            pltpu.VMEM((2, 1, TOK), F32),
            pltpu.VMEM((2 * EDGE, TOK, PAIR), F32),
            pltpu.VMEM((ROW, HEAD_DIM, TOK), F32),
            pltpu.VMEM((ROW, TOK, PAIR), BF),
            pltpu.VMEM((ROW, TOK, PAIR), BF),
            pltpu.VMEM((ROW, PAIR, TOK), BF),
            pltpu.VMEM((ROW, HEAD_DIM, TOK), BF),
            pltpu.VMEM((ROW, 8, TOK), F32),
            pltpu.VMEM(block(2 * EDGE), BF),
            pltpu.SemaphoreType.DMA((ROW + 4,)),
            pltpu.SemaphoreType.DMA((6,)),
        ],
        compiler_params=params(EDGE_MIB),
        cost_estimate=cost(9 * 10**9, 10 * 10**6),
    )(codes, arrived, edge, mate_edge, acc, tops)


def backward_near_kernel(
    codes, arrived, mate, e_in, att_in, dq_in, shares_in, g_t_in, edge_sum,
    od_out, d_own, d_mate,
    kv, qg, e, total, dq_sum, q_side, g_side, g_t, att, shares, od, d_out, sems, e_sems, out_sems,
):
    loads = [
        pltpu.make_async_copy(arrived.at[:, :, 1], qg, sems.at[0]),
        pltpu.make_async_copy(arrived.at[:, :, 0], kv.at[0:ROW], sems.at[1]),
        pltpu.make_async_copy(mate, kv.at[ROW:NEAR], sems.at[2]),
    ]
    loads.append(pltpu.make_async_copy(g_t_in, g_t, sems.at[2 * ROW + 1]))
    loads.append(pltpu.make_async_copy(shares_in, shares, sems.at[2 * ROW + 2]))
    later = [
        pltpu.make_async_copy(dq_in, dq_sum, sems.at[2 * ROW + 3]),
        pltpu.make_async_copy(att_in, att, sems.at[2 * ROW + 4]),
    ]

    def fetch(n, ring):
        j, b, _ = decode(codes, n)
        return pltpu.make_async_copy(e_in.at[j, b], e.at[ring], e_sems.at[ring])

    count = codes[NEAR_COUNT]
    fetch(0, 0).start()
    for load in loads + later:
        load.start()
    total[...] = jnp.zeros_like(total)
    for load in loads:
        load.wait()
    for x in range(ROW):
        qg_now = flat(qg.at[x])
        q_side[x] = query_side(qg_now)
        g_side[x] = jnp.where(low_lanes(), jnp.zeros_like(qg_now), qg_now)
    for load in later:
        load.wait()

    def one_pair(n, carry):
        ring = n % 2
        j, b, i = decode(codes, n)
        fetch(n, ring).wait()

        @pl.when(n + 1 < count)
        def _():
            fetch(n + 1, 1 - ring).start()

        share = shares[j, pl.ds(b, 1), :]
        dq, terms = backward_pair(flat(kv.at[i]), e[ring], share, g_t[j], q_side[j], g_side[j])
        total[i] += terms
        dq_sum[j] += dq
        return carry

    lax.fori_loop(0, count, one_pair, 0)
    outs = [
        pltpu.make_async_copy(d_out.at[ROW:NEAR], d_mate, out_sems.at[ROW]),
        pltpu.make_async_copy(d_out.at[0:ROW], d_own, out_sems.at[ROW + 1]),
    ]
    for x in range(ROW):
        outs.append(pltpu.make_async_copy(od.at[x], od_out.at[x], out_sems.at[x]))
    for i in range(ROW):
        d_out[ROW + i] = total[ROW + i].astype(BF).reshape(QUARTERS, PIECE, PAIR)
    outs[0].start()
    for i in range(ROW):
        d_out[i] = total[i].astype(BF).reshape(QUARTERS, PIECE, PAIR)
    outs[1].start()
    for x in range(ROW):
        both = jnp.concatenate([att[x], (dq_sum[x] * SCALE).astype(BF)], axis=0)
        od[x] = both.T.reshape(QUARTERS, PIECE, PAIR)
        outs[2 + x].start()
    for store in outs:
        store.wait()


def backward_near(codes, arrived, mate, e, att, dq, shares, g_t, edge_sum):
    return pl.pallas_call(
        backward_near_kernel,
        in_specs=[SMEM, ANY, ANY, HBM] + [ANY] * 5,
        out_specs=[ANY] * 3,
        out_shape=[shape(block(ROW))] * 3,
        scratch_shapes=[
            pltpu.VMEM(block(NEAR), BF),
            pltpu.VMEM(block(ROW), BF),
            pltpu.VMEM((2, TOK, TOK), BF),
            pltpu.VMEM((NEAR, TOK, PAIR), F32),
            pltpu.VMEM((ROW, HEAD_DIM, TOK), F32),
            pltpu.VMEM((ROW, TOK, PAIR), BF),
            pltpu.VMEM((ROW, TOK, PAIR), BF),
            pltpu.VMEM((ROW, PAIR, TOK), BF),
            pltpu.VMEM((ROW, HEAD_DIM, TOK), BF),
            pltpu.VMEM((ROW, 8, TOK), F32),
            pltpu.VMEM(block(ROW), BF),
            pltpu.VMEM(block(NEAR), BF),
            pltpu.SemaphoreType.DMA((2 * ROW + 5,)),
            pltpu.SemaphoreType.DMA((2,)),
            pltpu.SemaphoreType.DMA((ROW + 2,)),
        ],
        compiler_params=params(KERNEL_MIB),
        cost_estimate=cost(15 * 10**9, 20 * 10**6),
    )(codes, arrived, mate, e, att, dq, shares, g_t, edge_sum)


def fold_kernel(upper, own, got, edge_got, od, out, sums, sems, od_sem):
    kept = pltpu.make_async_copy(od, out.at[:, :, 1], od_sem)
    kept.start()
    stores = []
    for x in range(ROW):
        total = own[x].astype(F32) + got[x].astype(F32)
        listed = upper[0] == (0 if x >= EDGE else 1)
        far = edge_got[x % EDGE].astype(F32)
        sums[x] = (total + jnp.where(listed, far, jnp.zeros_like(far))).astype(BF)
        stores.append(pltpu.make_async_copy(sums.at[x], out.at[x, :, 0], sems.at[x]))
        stores[x].start()
    for store in stores:
        store.wait()
    kept.wait()


def fold(upper, own, got, edge_got, od):
    return pl.pallas_call(
        fold_kernel,
        in_specs=[SMEM, VMEM, VMEM, VMEM, ANY],
        out_specs=HBM,
        out_shape=shape((ROW, QUARTERS, 2, PIECE, PAIR)),
        scratch_shapes=[
            pltpu.VMEM(block(ROW), BF),
            pltpu.SemaphoreType.DMA((ROW,)),
            pltpu.SemaphoreType.DMA,
        ],
        compiler_params=params(16),
    )(upper, own, got, edge_got, od)


def block_rows(nbr_views, nbr_counts):
    z, x, c = lax.axis_index("z"), lax.axis_index("x"), lax.axis_index("c")
    at = nbr_views[0] % (4 * ROW)
    same_row = (at // NEAR) == (z % 2)
    column = (at // 2) % ROW
    place = jnp.where(same_row, column, NEAR + column % EDGE)
    place = place + jnp.where(at % 2 == c, 0, jnp.where(same_row, ROW, EDGE))
    mine = jnp.concatenate([x[None].astype(jnp.int32), place, nbr_counts + 1]).astype(jnp.int32)
    rows = [mine]
    for by in range(1, ROW):
        rows.append(lax.ppermute(mine, "x", [(i, (i - by) % ROW) for i in range(ROW)]))
    return x[None].astype(jnp.int32), jnp.stack(rows)


def local(queries, keys, values, out_grad, nbr_views, nbr_counts):
    x, rows_of_views = block_rows(nbr_views, nbr_counts)
    cores = [(0, 1), (1, 0)]
    rows = [(i, i ^ 1) for i in range(lax.axis_size("z"))]
    upper = lax.axis_index("z") % 2
    packed = pack(queries[0], keys[0], values[0], out_grad[0])
    arrived = lax.all_to_all(packed.reshape(HEADS, 2 * PIECE, PAIR), ("x", "y"), 0, 0, tiled=True)
    arrived, rows_of_views = lax.optimization_barrier((arrived, rows_of_views))
    arrived = arrived.reshape(ROW, QUARTERS, 2, PIECE, PAIR)
    start = jnp.where(upper == 1, 0, ROW - EDGE)
    edge = lax.ppermute(lax.dynamic_slice_in_dim(arrived, start, EDGE, 0)[:, :, 0], "z", rows)
    mate = lax.ppermute(arrived[:, :, 0], "c", cores)
    e, acc, tops, codes = forward_near(x, rows_of_views, arrived, mate)
    edge, acc = lax.optimization_barrier((edge, acc))
    mate_edge = lax.ppermute(edge, "c", cores)
    att, dq, shares, g_t, d_edge, d_mate_edge = edges(codes, arrived, edge, mate_edge, acc, tops)
    edge_sum = d_edge.astype(F32) + lax.ppermute(d_mate_edge, "c", cores).astype(F32)
    edge_sum = edge_sum.astype(BF)
    edge_got = lax.ppermute(edge_sum, "z", rows)
    od, d_own, d_mate = backward_near(codes, arrived, mate, e, att, dq, shares, g_t, edge_sum)
    d_mate, edge_got = lax.optimization_barrier((d_mate, edge_got))
    got = lax.ppermute(d_mate, "c", cores)
    out = fold(upper.astype(jnp.int32)[None], d_own, got, edge_got, od)
    back = lax.all_to_all(out.reshape(HEADS, 2 * PIECE, PAIR), ("x", "y"), 0, 0, tiled=True)
    results = unpack(back.reshape(HEADS, 2, PIECE, PAIR))
    return tuple(result[None] for result in results)


def solution(mesh):
    fine = Mesh(mesh.devices.reshape(8, 4, 2, 4), ("z", "x", "c", "y"))
    views = ("z", "x", "c")
    tokens = P(views, "y", None)
    return jax.shard_map(
        local,
        mesh=fine,
        in_specs=(tokens, tokens, tokens, tokens, P(views, None), P(views)),
        out_specs=(tokens, tokens, tokens, tokens),
        check_vma=False,
    )
```

```python
import jax
import jax.numpy as jnp
from jax import lax
from jax.experimental import pallas as pl
from jax.experimental.pallas import tpu as pltpu
from jax.sharding import Mesh, PartitionSpec as P

HEAD_DIM = 64
PAIR = 2 * HEAD_DIM
HEADS = 16
WIDTH = HEADS * HEAD_DIM
TOK = 768
PIECE = 192
QUARTERS = TOK // PIECE
ROW = 4
EDGE = 2
NEAR = 2 * ROW
MAXNB = 3
SLOTS = 1 + MAXNB
SUMS = HEAD_DIM + 16
TOP = HEAD_DIM + 8
CODES = 32
NEAR_COUNT = CODES - 2
EDGE_COUNT = CODES - 1
KERNEL_MIB = 48
EDGE_MIB = 48
SCALE = HEAD_DIM ** (-0.5)
BF = jnp.bfloat16
F32 = jnp.float32

ANY = pl.BlockSpec(memory_space=pl.ANY)
HBM = pl.BlockSpec(memory_space=pltpu.HBM)
SMEM = pl.BlockSpec(memory_space=pltpu.SMEM)
VMEM = pl.BlockSpec(memory_space=pltpu.VMEM)


def params(mib):
    return pltpu.CompilerParams(vmem_limit_bytes=mib * 1024 * 1024)


def shape(dims, dtype=BF):
    return jax.ShapeDtypeStruct(dims, dtype)


def cost(flops, moved):
    return pl.CostEstimate(flops=flops, bytes_accessed=moved, transcendentals=0)


def block(*lead):
    return lead + (QUARTERS, PIECE, PAIR)


def pack_kernel(q_ref, k_ref, v_ref, g_ref, out_ref):
    for side, (a, b) in enumerate(((k_ref, v_ref), (q_ref, g_ref))):
        for h in range(HEADS):
            cols = slice(h * HEAD_DIM, (h + 1) * HEAD_DIM)
            out_ref[h, side] = jnp.concatenate([a[:, cols], b[:, cols]], axis=1)


def pack(*arrays):
    steps = 2
    return pl.pallas_call(
        pack_kernel,
        grid=(steps,),
        in_specs=[pl.BlockSpec((PIECE // steps, WIDTH), lambda i: (i, 0))] * 4,
        out_specs=pl.BlockSpec((HEADS, 2, PIECE // steps, PAIR), lambda i: (0, 0, i, 0)),
        out_shape=shape((HEADS, 2, PIECE, PAIR)),
        compiler_params=params(60),
    )(*arrays)


def unpack_kernel(in_ref, a_ref, q_ref, k_ref, v_ref, a, q, k, v, sems):
    stores = []
    for side, pairs in enumerate((((k, k_ref), (v, v_ref)), ((a, a_ref), (q, q_ref)))):
        for h in range(HEADS):
            cols = slice(h * HEAD_DIM, (h + 1) * HEAD_DIM)
            pairs[0][0][:, cols] = in_ref[h, side, :, :HEAD_DIM]
            pairs[1][0][:, cols] = in_ref[h, side, :, HEAD_DIM:]
        for scratch, out in pairs:
            stores.append(pltpu.make_async_copy(scratch, out, sems.at[len(stores)]))
            stores[-1].start()
    for store in stores:
        store.wait()


def unpack(packed):
    return pl.pallas_call(
        unpack_kernel,
        in_specs=[VMEM],
        out_specs=[HBM] * 4,
        out_shape=[shape((PIECE, WIDTH))] * 4,
        scratch_shapes=[pltpu.VMEM((PIECE, WIDTH), BF)] * 4 + [pltpu.SemaphoreType.DMA((4,))],
        compiler_params=params(16),
    )(packed)


def dot(a, b):
    return jnp.dot(a, b, preferred_element_type=F32)


def dot_nt(a, b):
    return lax.dot_general(a, b, (((1,), (1,)), ((), ())), preferred_element_type=F32)


def flat(ref):
    return ref[...].reshape(TOK, PAIR)


def low_lanes():
    return lax.broadcasted_iota(jnp.int32, (TOK, PAIR), 1) < HEAD_DIM


def query_side(qg):
    return jnp.where(low_lanes(), qg * SCALE, jnp.zeros_like(qg)).astype(BF)


def scores_of(kv, q_side):
    scores = dot_nt(kv, q_side)
    return scores, jnp.max(scores, axis=0, keepdims=True)


def values_of(kv, scores, top):
    e = jnp.exp(scores - top).astype(BF)
    left = jnp.concatenate([kv.T[HEAD_DIM:], jnp.ones((16, TOK), BF)], axis=0)
    part = dot(left, e)
    return e, jnp.concatenate([part[:TOP], jnp.broadcast_to(top, (8, TOK))], axis=0)


def grad_rows(qg_t, delta):
    d_hi = delta.astype(BF)
    rest = delta - d_hi.astype(F32)
    d_mid = rest.astype(BF)
    d_lo = (rest - d_mid.astype(F32)).astype(BF)
    sub = lax.broadcasted_iota(jnp.int32, (PAIR, TOK), 0)
    low = jnp.where(sub == 0, -d_hi, jnp.where(sub == 1, -d_mid, jnp.where(sub == 2, -d_lo, jnp.zeros_like(qg_t))))
    return jnp.where(sub < HEAD_DIM, low, qg_t)


def backward_pair(kv, e, share, g_t, q_side, g_side):
    dprobs = dot(jnp.where(low_lanes(), jnp.ones_like(kv), kv), g_t)
    p = e.astype(F32) * share
    ds = (p * dprobs).astype(BF)
    dq = dot(kv.T[:HEAD_DIM], ds)
    return dq, dot(jnp.concatenate([ds, p.astype(BF)], axis=1), jnp.concatenate([q_side, g_side], axis=0))


def decode(codes, n):
    code = codes[n]
    return code >> 6, (code >> 4) & 3, code & 15


def list_pairs(x, rows, codes):
    n = jnp.int32(0)
    for kind in range(2):
        for t in range(ROW):
            view = (x + t) & (ROW - 1)
            for b in range(SLOTS):
                place = rows[t, b]
                codes[n] = view * 64 + b * 16 + place
                wanted = place < NEAR if kind == 0 else place >= NEAR
                n = n + jnp.where(jnp.logical_and(b < rows[t, SLOTS], wanted), 1, 0)
        if kind == 0:
            near = n
    codes[NEAR_COUNT] = near
    codes[EDGE_COUNT] = n - near


def merge(acc, j, part, top):
    old_top = acc[j, TOP : TOP + 1]
    new_top = jnp.maximum(old_top, top)
    acc[j, :TOP] = acc[j, :TOP] * jnp.exp(old_top - new_top) + part[:TOP] * jnp.exp(top - new_top)
    acc[j, TOP:] = jnp.broadcast_to(new_top, (8, TOK))


def forward_near_kernel(
    x_ref, rows, arrived, mate, e_out, acc_out, tops_out, codes,
    kv, qg, q_side, scores, top_now, e, acc, tops, sems, e_sems, out_sems,
):
    loads = [
        pltpu.make_async_copy(arrived.at[:, :, 1], qg, sems.at[0]),
        pltpu.make_async_copy(arrived.at[:, :, 0], kv.at[0:ROW], sems.at[1]),
        pltpu.make_async_copy(mate, kv.at[ROW:NEAR], sems.at[2]),
    ]
    for load in loads:
        load.start()
    list_pairs(x_ref[0], rows, codes)
    acc[...] = jnp.zeros_like(acc)
    for x in range(ROW):
        acc[x, TOP:] = jnp.full((8, TOK), -jnp.inf, F32)
    for load in loads:
        load.wait()
    for x in range(ROW):
        q_side[x] = query_side(flat(qg.at[x]))

    def store(j, b, ring):
        return pltpu.make_async_copy(e.at[ring], e_out.at[j, b], e_sems.at[ring])

    def score(n, ring):
        j, _, i = decode(codes, n)
        scores[ring], top_now[ring] = scores_of(flat(kv.at[i]), q_side[j])

    count = codes[NEAR_COUNT]
    score(0, 0)

    def one_pair(n, following):
        ring = n % 2
        j, b, i = decode(codes, n)

        @pl.when(n >= 2)
        def _():
            store(j, b, ring).wait()

        top = top_now[ring]
        e[ring], part = values_of(flat(kv.at[i]), scores[ring], top)
        if following:
            score(n + 1, 1 - ring)
        merge(acc, j, part, top)
        tops[j, pl.ds(b, 1), :] = top
        store(j, b, ring).start()

    def step(n, carry):
        one_pair(n, True)
        return carry

    lax.fori_loop(0, count - 1, step, 0)
    one_pair(count - 1, False)
    outs = [
        pltpu.make_async_copy(acc, acc_out, out_sems.at[0]),
        pltpu.make_async_copy(tops, tops_out, out_sems.at[1]),
    ]
    for out in outs:
        out.start()
    for ring in range(2):
        store(0, 0, ring).wait()
    for out in outs:
        out.wait()


def forward_near(x, rows, arrived, mate):
    return pl.pallas_call(
        forward_near_kernel,
        in_specs=[SMEM] * 2 + [ANY] * 2,
        out_specs=[HBM, ANY, ANY, SMEM],
        out_shape=[
            shape((ROW, SLOTS, TOK, TOK)),
            shape((ROW, SUMS, TOK), F32),
            shape((ROW, 8, TOK), F32),
            shape((CODES,), jnp.int32),
        ],
        scratch_shapes=[
            pltpu.VMEM(block(NEAR), BF),
            pltpu.VMEM(block(ROW), BF),
            pltpu.VMEM((ROW, TOK, PAIR), BF),
            pltpu.VMEM((2, TOK, TOK), F32),
            pltpu.VMEM((2, 1, TOK), F32),
            pltpu.VMEM((2, TOK, TOK), BF),
            pltpu.VMEM((ROW, SUMS, TOK), F32),
            pltpu.VMEM((ROW, 8, TOK), F32),
            pltpu.SemaphoreType.DMA((2 * ROW + 1,)),
            pltpu.SemaphoreType.DMA((2,)),
            pltpu.SemaphoreType.DMA((2,)),
        ],
        compiler_params=params(KERNEL_MIB),
        cost_estimate=cost(9 * 10**9, 20 * 10**6),
    )(x, rows, arrived, mate)


def edge_kernel(
    codes, arrived, edge, mate_edge, acc_in, tops_in,
    att_out, dq_out, shares_out, g_t_out, d_edge, d_mate_edge,
    kv, qg, acc, tops, e, scores, top_now, total, dq_sum, q_side, g_side, g_t, att, shares, d_out, sems, out_sems,
):
    loads = [pltpu.make_async_copy(arrived.at[:, :, 1], qg, sems.at[0])]
    loads.append(pltpu.make_async_copy(edge, kv.at[0:EDGE], sems.at[ROW]))
    loads.append(pltpu.make_async_copy(mate_edge, kv.at[EDGE : 2 * EDGE], sems.at[ROW + 1]))
    loads.append(pltpu.make_async_copy(acc_in, acc, sems.at[ROW + 2]))
    loads.append(pltpu.make_async_copy(tops_in, tops, sems.at[ROW + 3]))
    for load in loads:
        load.start()
    total[...] = jnp.zeros_like(total)
    dq_sum[...] = jnp.zeros_like(dq_sum)
    for load in loads:
        load.wait()
    for x in range(ROW):
        qg_now = flat(qg.at[x])
        q_side[x] = query_side(qg_now)
        g_side[x] = jnp.where(low_lanes(), jnp.zeros_like(qg_now), qg_now)

    first, count = codes[NEAR_COUNT], codes[EDGE_COUNT]

    def score(n, ring):
        j, _, i = decode(codes, first + n)
        scores[ring], top_now[ring] = scores_of(flat(kv.at[i - NEAR]), q_side[j])

    @pl.when(count > 0)
    def _():
        score(0, 0)

    def one_forward(n, carry):
        ring = n % 2
        j, b, i = decode(codes, first + n)
        top = top_now[ring]
        e[n], part = values_of(flat(kv.at[i - NEAR]), scores[ring], top)
        score(jnp.minimum(n + 1, count - 1), 1 - ring)
        merge(acc, j, part, top)
        tops[j, pl.ds(b, 1), :] = top
        return carry

    lax.fori_loop(0, count, one_forward, 0)

    for j in range(ROW):
        inverse = 1.0 / acc[j, HEAD_DIM : HEAD_DIM + 1]
        att_now = acc[j, :HEAD_DIM] * inverse
        qg_t = flat(qg.at[j]).T
        delta = jnp.sum(qg_t[HEAD_DIM:].astype(F32) * att_now, axis=0, keepdims=True)
        att[j] = att_now.astype(BF)
        shares[j] = jnp.exp(tops[j] - acc[j, TOP : TOP + 1]) * inverse
        g_t[j] = grad_rows(qg_t, delta)

    early = [
        pltpu.make_async_copy(att, att_out, out_sems.at[0]),
        pltpu.make_async_copy(shares, shares_out, out_sems.at[1]),
        pltpu.make_async_copy(g_t, g_t_out, out_sems.at[2]),
    ]
    for out in early:
        out.start()

    def one_backward(n, carry):
        j, b, i = decode(codes, first + n)
        share = shares[j, pl.ds(b, 1), :]
        dq, terms = backward_pair(flat(kv.at[i - NEAR]), e[n], share, g_t[j], q_side[j], g_side[j])
        total[i - NEAR] += terms
        dq_sum[j] += dq
        return carry

    lax.fori_loop(0, count, one_backward, 0)
    for i in range(2 * EDGE):
        d_out[i] = total[i].astype(BF).reshape(QUARTERS, PIECE, PAIR)
    late = [
        pltpu.make_async_copy(d_out.at[0:EDGE], d_edge, out_sems.at[3]),
        pltpu.make_async_copy(d_out.at[EDGE : 2 * EDGE], d_mate_edge, out_sems.at[4]),
        pltpu.make_async_copy(dq_sum, dq_out, out_sems.at[5]),
    ]
    for out in late:
        out.start()
    for out in early + late:
        out.wait()


def edges(codes, arrived, edge, mate_edge, acc, tops):
    return pl.pallas_call(
        edge_kernel,
        in_specs=[SMEM] + [ANY] * 5,
        out_specs=[ANY] * 6,
        out_shape=[
            shape((ROW, HEAD_DIM, TOK)),
            shape((ROW, HEAD_DIM, TOK), F32),
            shape((ROW, 8, TOK), F32),
            shape((ROW, PAIR, TOK)),
            shape(block(EDGE)),
            shape(block(EDGE)),
        ],
        scratch_shapes=[
            pltpu.VMEM(block(2 * EDGE), BF),
            pltpu.VMEM(block(ROW), BF),
            pltpu.VMEM((ROW, SUMS, TOK), F32),
            pltpu.VMEM((ROW, 8, TOK), F32),
            pltpu.VMEM((ROW * MAXNB, TOK, TOK), BF),
            pltpu.VMEM((2, TOK, TOK), F32),
            pltpu.VMEM((2, 1, TOK), F32),
            pltpu.VMEM((2 * EDGE, TOK, PAIR), F32),
            pltpu.VMEM((ROW, HEAD_DIM, TOK), F32),
            pltpu.VMEM((ROW, TOK, PAIR), BF),
            pltpu.VMEM((ROW, TOK, PAIR), BF),
            pltpu.VMEM((ROW, PAIR, TOK), BF),
            pltpu.VMEM((ROW, HEAD_DIM, TOK), BF),
            pltpu.VMEM((ROW, 8, TOK), F32),
            pltpu.VMEM(block(2 * EDGE), BF),
            pltpu.SemaphoreType.DMA((ROW + 4,)),
            pltpu.SemaphoreType.DMA((6,)),
        ],
        compiler_params=params(EDGE_MIB),
        cost_estimate=cost(9 * 10**9, 10 * 10**6),
    )(codes, arrived, edge, mate_edge, acc, tops)


def backward_near_kernel(
    codes, arrived, mate, e_in, att_in, dq_in, shares_in, g_t_in,
    od_out, d_own, d_mate,
    kv, qg, e, total, dq_sum, q_side, g_side, g_t, att, shares, od, d_out, sems, e_sems, out_sems,
):
    loads = [
        pltpu.make_async_copy(arrived.at[:, :, 1], qg, sems.at[0]),
        pltpu.make_async_copy(arrived.at[:, :, 0], kv.at[0:ROW], sems.at[1]),
        pltpu.make_async_copy(mate, kv.at[ROW:NEAR], sems.at[2]),
    ]
    loads.append(pltpu.make_async_copy(g_t_in, g_t, sems.at[2 * ROW + 1]))
    loads.append(pltpu.make_async_copy(shares_in, shares, sems.at[2 * ROW + 2]))
    later = [
        pltpu.make_async_copy(dq_in, dq_sum, sems.at[2 * ROW + 3]),
        pltpu.make_async_copy(att_in, att, sems.at[2 * ROW + 4]),
    ]

    def fetch(n, ring):
        j, b, _ = decode(codes, n)
        return pltpu.make_async_copy(e_in.at[j, b], e.at[ring], e_sems.at[ring])

    count = codes[NEAR_COUNT]
    fetch(0, 0).start()
    for load in loads + later:
        load.start()
    total[...] = jnp.zeros_like(total)
    for load in loads:
        load.wait()
    for x in range(ROW):
        qg_now = flat(qg.at[x])
        q_side[x] = query_side(qg_now)
        g_side[x] = jnp.where(low_lanes(), jnp.zeros_like(qg_now), qg_now)
    for load in later:
        load.wait()

    def one_pair(n, carry):
        ring = n % 2
        j, b, i = decode(codes, n)
        fetch(n, ring).wait()

        @pl.when(n + 1 < count)
        def _():
            fetch(n + 1, 1 - ring).start()

        share = shares[j, pl.ds(b, 1), :]
        dq, terms = backward_pair(flat(kv.at[i]), e[ring], share, g_t[j], q_side[j], g_side[j])
        total[i] += terms
        dq_sum[j] += dq
        return carry

    lax.fori_loop(0, count, one_pair, 0)
    outs = [
        pltpu.make_async_copy(d_out.at[ROW:NEAR], d_mate, out_sems.at[ROW]),
        pltpu.make_async_copy(d_out.at[0:ROW], d_own, out_sems.at[ROW + 1]),
    ]
    for x in range(ROW):
        outs.append(pltpu.make_async_copy(od.at[x], od_out.at[x], out_sems.at[x]))
    for i in range(ROW):
        d_out[ROW + i] = total[ROW + i].astype(BF).reshape(QUARTERS, PIECE, PAIR)
    outs[0].start()
    for i in range(ROW):
        d_out[i] = total[i].astype(BF).reshape(QUARTERS, PIECE, PAIR)
    outs[1].start()
    for x in range(ROW):
        both = jnp.concatenate([att[x], (dq_sum[x] * SCALE).astype(BF)], axis=0)
        od[x] = both.T.reshape(QUARTERS, PIECE, PAIR)
        outs[2 + x].start()
    for store in outs:
        store.wait()


def backward_near(codes, arrived, mate, e, att, dq, shares, g_t):
    return pl.pallas_call(
        backward_near_kernel,
        in_specs=[SMEM, ANY, ANY, HBM] + [ANY] * 4,
        out_specs=[ANY] * 3,
        out_shape=[shape(block(ROW))] * 3,
        scratch_shapes=[
            pltpu.VMEM(block(NEAR), BF),
            pltpu.VMEM(block(ROW), BF),
            pltpu.VMEM((2, TOK, TOK), BF),
            pltpu.VMEM((NEAR, TOK, PAIR), F32),
            pltpu.VMEM((ROW, HEAD_DIM, TOK), F32),
            pltpu.VMEM((ROW, TOK, PAIR), BF),
            pltpu.VMEM((ROW, TOK, PAIR), BF),
            pltpu.VMEM((ROW, PAIR, TOK), BF),
            pltpu.VMEM((ROW, HEAD_DIM, TOK), BF),
            pltpu.VMEM((ROW, 8, TOK), F32),
            pltpu.VMEM(block(ROW), BF),
            pltpu.VMEM(block(NEAR), BF),
            pltpu.SemaphoreType.DMA((2 * ROW + 5,)),
            pltpu.SemaphoreType.DMA((2,)),
            pltpu.SemaphoreType.DMA((ROW + 2,)),
        ],
        compiler_params=params(KERNEL_MIB),
        cost_estimate=cost(15 * 10**9, 20 * 10**6),
    )(codes, arrived, mate, e, att, dq, shares, g_t)


def fold_kernel(upper, own, got, edge_got, mate_edge_got, od, out, sums, sems, od_sem):
    kept = pltpu.make_async_copy(od, out.at[:, :, 1], od_sem)
    kept.start()
    stores = []
    for x in range(ROW):
        total = own[x].astype(F32) + got[x].astype(F32)
        listed = upper[0] == (0 if x >= EDGE else 1)
        far = edge_got[x % EDGE].astype(F32) + mate_edge_got[x % EDGE].astype(F32)
        sums[x] = (total + jnp.where(listed, far, jnp.zeros_like(far))).astype(BF)
        stores.append(pltpu.make_async_copy(sums.at[x], out.at[x, :, 0], sems.at[x]))
        stores[x].start()
    for store in stores:
        store.wait()
    kept.wait()


def fold(upper, own, got, edge_got, mate_edge_got, od):
    return pl.pallas_call(
        fold_kernel,
        in_specs=[SMEM, VMEM, VMEM, VMEM, VMEM, ANY],
        out_specs=HBM,
        out_shape=shape((ROW, QUARTERS, 2, PIECE, PAIR)),
        scratch_shapes=[
            pltpu.VMEM(block(ROW), BF),
            pltpu.SemaphoreType.DMA((ROW,)),
            pltpu.SemaphoreType.DMA,
        ],
        compiler_params=params(16),
    )(upper, own, got, edge_got, mate_edge_got, od)


def block_rows(nbr_views, nbr_counts):
    z, x, c = lax.axis_index("z"), lax.axis_index("x"), lax.axis_index("c")
    at = nbr_views[0] % (4 * ROW)
    same_row = (at // NEAR) == (z % 2)
    column = (at // 2) % ROW
    place = jnp.where(same_row, column, NEAR + column % EDGE)
    place = place + jnp.where(at % 2 == c, 0, jnp.where(same_row, ROW, EDGE))
    mine = jnp.concatenate([x[None].astype(jnp.int32), place, nbr_counts + 1]).astype(jnp.int32)
    rows = [mine]
    for by in range(1, ROW):
        rows.append(lax.ppermute(mine, "x", [(i, (i - by) % ROW) for i in range(ROW)]))
    return x[None].astype(jnp.int32), jnp.stack(rows)


def local(queries, keys, values, out_grad, nbr_views, nbr_counts):
    x, rows_of_views = block_rows(nbr_views, nbr_counts)
    cores = [(0, 1), (1, 0)]
    rows = [(i, i ^ 1) for i in range(lax.axis_size("z"))]
    upper = lax.axis_index("z") % 2
    packed = pack(queries[0], keys[0], values[0], out_grad[0])
    arrived = lax.all_to_all(packed.reshape(HEADS, 2 * PIECE, PAIR), ("x", "y"), 0, 0, tiled=True)
    arrived, rows_of_views = lax.optimization_barrier((arrived, rows_of_views))
    arrived = arrived.reshape(ROW, QUARTERS, 2, PIECE, PAIR)
    start = jnp.where(upper == 1, 0, ROW - EDGE)
    edge = lax.ppermute(lax.dynamic_slice_in_dim(arrived, start, EDGE, 0)[:, :, 0], "z", rows)
    mate = lax.ppermute(arrived[:, :, 0], "c", cores)
    e, acc, tops, codes = forward_near(x, rows_of_views, arrived, mate)
    edge, acc = lax.optimization_barrier((edge, acc))
    mate_edge = lax.ppermute(edge, "c", cores)
    att, dq, shares, g_t, d_edge, d_mate_edge = edges(codes, arrived, edge, mate_edge, acc, tops)
    edge_got = lax.ppermute(d_edge, "z", rows)
    across = [(2 * i + c, 2 * (i ^ 1) + 1 - c) for i in range(lax.axis_size("z")) for c in range(2)]
    mate_edge_got = lax.ppermute(d_mate_edge, ("z", "c"), across)
    od, d_own, d_mate = backward_near(codes, arrived, mate, e, att, dq, shares, g_t)
    d_mate, edge_got, mate_edge_got = lax.optimization_barrier((d_mate, edge_got, mate_edge_got))
    got = lax.ppermute(d_mate, "c", cores)
    out = fold(upper.astype(jnp.int32)[None], d_own, got, edge_got, mate_edge_got, od)
    back = lax.all_to_all(out.reshape(HEADS, 2 * PIECE, PAIR), ("x", "y"), 0, 0, tiled=True)
    results = unpack(back.reshape(HEADS, 2, PIECE, PAIR))
    return tuple(result[None] for result in results)


def solution(mesh):
    fine = Mesh(mesh.devices.reshape(8, 4, 2, 4), ("z", "x", "c", "y"))
    views = ("z", "x", "c")
    tokens = P(views, "y", None)
    return jax.shard_map(
        local,
        mesh=fine,
        in_specs=(tokens, tokens, tokens, tokens, P(views, None), P(views)),
        out_specs=(tokens, tokens, tokens, tokens),
        check_vma=False,
    )
```
